32 devices in a mesh: col: 8 (over y, x, core), sec: 4 (over z).
Axes of the slice: x: 2, y: 2, z: 4, core: 2. Of those that a mesh axis runs over, the one named last changes fastest.
Arguments:
- couplings: float32 [2, 8, 3, 64, 512], P(None, 'col', None, None, 'sec'), may hold values from -0.625 to 0.625
- lower_sites: float32 [2, 8, 128, 128], P(None, 'col'), may hold values from -1.5 to 1.5
- left_edge: float32 [2, 8, 64, 128], P(None, 'sec'), may hold values from -6 to 6
- right_edge: float32 [2, 8, 64, 128], P(None, 'sec'), may hold values from -6 to 6
- bond_sizes: int32 [8, 8], P('col', 'sec'), may hold values from 1 to 64, as said below
Outputs:
- coupling_grad: float32 [2, 8, 3, 64, 512], P(None, 'col', None, None, 'sec')
The draws below stay inside these ranges and needn't reach their ends.
Inputs may be any that keep to these rules, and one draw needn't show every extreme that they name: bond_sizes[c, q] is the number of live rows of sector q of the bond right of column c; some entry equals 64.
All inputs are finite; a program needn't handle non-finite values.
Results may differ from the reference program's by a relative error of at most 0.0003.
Values sent between devices are 32-bit elements; how exact they have to be, the bound alone decides.
A program may use at most 64 MiB of HBM per device.

```python
import math
import jax
import jax.numpy as jnp
from jax import lax

BLK = 64
W = 128
ROWS = 2
SECTORS = 8
NCOL = 8


def draw_bond_sizes(key, part):
    first, second, third = jax.random.split(key, 3)
    values = jax.random.randint(first, (NCOL, SECTORS), 1, BLK + 1)
    column_pick = jax.random.randint(second, (), 0, NCOL)
    sector_pick = jax.random.randint(third, (), 0, SECTORS)
    return values.at[column_pick, sector_pick].set(BLK).astype(jnp.int32)


def draw_lower_sites(key, part):
    first, second = jax.random.split(key)
    full_shape = (ROWS, NCOL, W, W)
    identity = (lax.broadcasted_iota(jnp.int32, (W, W), 0) == lax.broadcasted_iota(jnp.int32, (W, W), 1)).astype(jnp.float32)
    spread = 0.3
    low_diag = 0.75
    high_diag = 1.25
    noise = jax.random.truncated_normal(first, -4.0, 4.0, full_shape, jnp.float32)
    diagonal = jax.random.uniform(second, (ROWS, NCOL, 1, W), jnp.float32, low_diag, high_diag)
    mean_square = ((low_diag + high_diag) / 2.0) ** 2 + (high_diag - low_diag) ** 2 / 12.0
    factor = 1.0 / math.sqrt(mean_square + spread * spread)
    values = factor * (identity * diagonal + spread / math.sqrt(W) * noise)
    return values.astype(jnp.float32)


def block_scale(key, dims, pieces, least, high):
    loudness, own = 1.0, jax.random.fold_in(key, 6)
    for axis_at, parts in pieces:
        draws = jnp.exp(jax.random.uniform(jax.random.fold_in(own, axis_at), (parts,), jnp.float32, least / len(pieces), high / len(pieces)))
        loudness = loudness * jnp.repeat(draws, dims[axis_at] // parts).reshape([-1 if axis == axis_at else 1 for axis in range(len(dims))])
    return loudness


def centred(key, shape, deviation, bound, cuts=(), kind=jnp.bfloat16):
    array = jax.random.normal(key, shape, jnp.float32) * deviation
    if len(cuts) > 0:
        array = block_scale(key, shape, cuts, -0.22, 0.18) * array
    return jnp.clip(array, min=-bound, max=bound).astype(kind)


def setup_inputs(seed: int = 0) -> dict:
    streams_of = jax.random.split(jax.random.key(seed), 6)
    couplings = centred(streams_of[0], (ROWS, NCOL, 3, BLK, SECTORS * BLK), (3 * BLK // 2) ** -0.5, 0.625, ((1, 8), (4, 4)), jnp.float32)
    lower_sites = draw_lower_sites(jax.random.fold_in(streams_of[5], 71), 0)
    left_edge = centred(streams_of[2], (ROWS, SECTORS, BLK, W), 1.0, 6.0, ((1, 4),), jnp.float32)
    right_edge = centred(streams_of[3], (ROWS, SECTORS, BLK, W), 1.0, 6.0, ((1, 4),), jnp.float32)
    bond_sizes = draw_bond_sizes(jax.random.fold_in(streams_of[5], 71), 0)
    return {"couplings": couplings, "lower_sites": lower_sites, "left_edge": left_edge, "right_edge": right_edge, "bond_sizes": bond_sizes}


HIGHEST = lax.Precision.HIGHEST

def live_mask(sizes_row):
    positions = lax.broadcasted_iota(jnp.int32, (sizes_row.shape[0], BLK), 1)
    return (positions < sizes_row[:, None]).astype(jnp.float32)[:, :, None]

def reference(couplings, lower_sites, left_edge, right_edge, bond_sizes):
    blocks_all = couplings.reshape(ROWS, NCOL, 3, BLK, SECTORS, BLK)
    zeros_block = jnp.zeros((ROWS, 1, BLK, W), jnp.float32)
    scale_factor = 1.0 / math.sqrt(W)
    travel = left_edge
    lefts = []
    for column in range(NCOL):
        lefts.append(travel)
        products = jnp.einsum('rpiqj,rqjw->rpqiw', blocks_all[:, column], travel, precision=HIGHEST)
        from_below = jnp.concatenate([zeros_block, products[:, 2, :-1]], axis=1)
        from_above = jnp.concatenate([products[:, 0, 1:], zeros_block], axis=1)
        summed = products[:, 1] + from_below + from_above
        travel = jnp.einsum('rqiw,rwv->rqiv', summed, lower_sites[:, column], precision=HIGHEST) * live_mask(bond_sizes[column])[None]
    travel = right_edge
    grads = [None] * NCOL
    for column in reversed(range(NCOL)):
        masked = travel * live_mask(bond_sizes[column])[None]
        images = jnp.einsum('rqiw,rvw->rqiv', masked, lower_sites[:, column], precision=HIGHEST)
        padded = jnp.concatenate([zeros_block, images, zeros_block], axis=1)
        shifted = jnp.stack([padded[:, 0:SECTORS], padded[:, 1:SECTORS + 1], padded[:, 2:SECTORS + 2]], axis=1)
        gradient = jnp.einsum('rpqiw,rqjw->rpiqj', shifted, lefts[column], precision=HIGHEST) * scale_factor
        grads[column] = gradient.reshape(ROWS, 3, BLK, SECTORS * BLK)
        travel = jnp.einsum('rpiqj,rpqiw->rqjw', blocks_all[:, column], shifted, precision=HIGHEST)
    return jnp.stack(grads, axis=1)
```

```python
import functools
import math

import jax
import jax.numpy as jnp
from jax import lax
from jax.experimental import pallas as pl
from jax.experimental.pallas import tpu as pltpu
from jax.sharding import PartitionSpec as P

MESH = pl.DeviceIdType.MESH
F32 = jnp.float32
BF16 = jnp.bfloat16


def split(x):
    high = x.astype(BF16)
    low = (x - high.astype(F32)).astype(BF16)
    return high, low


def wide(x):
    return jnp.concatenate(split(x), axis=1)


def dot(a, b, contract):
    return lax.dot_general(a, b, (contract, ((), ())), preferred_element_type=F32)


def times(x_wide, y):
    pair = wide(y)
    both = dot(x_wide, jnp.concatenate([pair, pair], axis=0), ((1,), (0,)))
    n = y.shape[1]
    return both[:, :n] + both[:, n:]


def times_t(x_wide, y):
    high, low = split(y)
    rows = jnp.concatenate(
        [jnp.concatenate([high, high], axis=1), jnp.concatenate([low, low], axis=1)], axis=0
    )
    both = dot(x_wide, rows, ((1,), (1,)))
    n = y.shape[0]
    return both[:, :n] + both[:, n:]


def kernel(
    cols, secs, a_ref, b_ref, left_ref, right_ref, size_ref, out_ref,
    l_in, r_in, l_out, r_out, m_keep, x_keep, y_keep, a_wide, at_tall, weight, sizes, halo_sizes, prods, others,
    l_send, l_recv, r_send, r_recv, h_send, h_recv, k_send, k_recv,
):
    row_count = a_ref.shape[0]
    blk = a_ref.shape[3]
    width = b_ref.shape[3]
    rounds = cols.bit_length() - 1
    c = lax.axis_index("col")
    s = lax.axis_index("sec")
    below, above = s > 0, s < secs - 1
    before, after = c > 0, c < cols - 1
    low_rows, mid_rows, high_rows = pl.ds(0, blk), pl.ds(blk, 2 * blk), pl.ds(3 * blk, blk)

    def copy(src, dst, send, recv, dc, ds):
        return pltpu.make_async_remote_copy(
            src_ref=src, dst_ref=dst, send_sem=send, recv_sem=recv,
            device_id=(dc, ds), device_id_type=MESH,
        )

    barrier = pltpu.get_barrier_semaphore()
    count = jnp.int32(rounds)
    for k in range(rounds):
        partner = c + (1 << k) * (1 - 2 * ((c // (1 << k)) % 2))
        pl.semaphore_signal(barrier, inc=1, device_id=(partner, s), device_id_type=MESH)
    for dc, there in ((0, None), (-1, before), (1, after)):
        for ds, beside in ((0, None), (-1, below), (1, above)):
            if dc == 0 and ds == 0:
                continue
            if there is None:
                exists = beside
            elif beside is None:
                exists = there
            else:
                exists = there & beside
            count = count + exists.astype(jnp.int32)

            @pl.when(exists)
            def _(dc=dc, ds=ds):
                pl.semaphore_signal(barrier, inc=1, device_id=(c + dc, s + ds), device_id_type=MESH)

    sizes[0:8, :] = jnp.full((8, width), size_ref[0, 0].astype(F32), F32)
    sizes[8:16, :] = jnp.full((8, width), size_ref[0, 1].astype(F32), F32)
    norms = []
    for r in range(row_count):
        lower = b_ref[r, 0]
        norm = jnp.max(jnp.sum(jnp.abs(lower), axis=1, keepdims=True), axis=0, keepdims=True)
        norm = jnp.maximum(norm, 1e-30)
        norms.append(norm)
        prods[0, r] = lower / norm

    @pl.when(s == 0)
    def _():
        halo_sizes[0:8, :] = jnp.zeros((8, width), F32)
        r_in[:, low_rows, :] = jnp.zeros((row_count, blk, width), F32)
        l_in[:, low_rows, :] = jnp.zeros((row_count, blk, width), F32)

    @pl.when(s == secs - 1)
    def _():
        halo_sizes[8:16, :] = jnp.zeros((8, width), F32)
        r_in[:, high_rows, :] = jnp.zeros((row_count, blk, width), F32)
        l_in[:, high_rows, :] = jnp.zeros((row_count, blk, width), F32)

    pl.semaphore_wait(barrier, count)

    def size_up():
        return copy(sizes.at[8:16], halo_sizes.at[0:8], h_send.at[0], h_recv.at[0], c, s + 1)

    def size_down():
        return copy(sizes.at[0:8], halo_sizes.at[8:16], h_send.at[1], h_recv.at[1], c, s - 1)

    def right_copies(r, src, dc):
        return (
            copy(src.at[pl.ds(0, 2 * blk)], r_in.at[r, mid_rows], r_send.at[r, 0], r_recv.at[r, 0], dc, s),
            copy(src.at[pl.ds(0, blk)], r_in.at[r, high_rows], r_send.at[r, 1], r_recv.at[r, 1], dc, s - 1),
            copy(src.at[pl.ds(blk, blk)], r_in.at[r, low_rows], r_send.at[r, 2], r_recv.at[r, 2], dc, s + 1),
        )

    def left_copies(r):
        src = l_out.at[r]
        return (
            copy(src.at[mid_rows], l_in.at[r, mid_rows], l_send.at[r, 0], l_recv.at[r, 0], c + 1, s),
            copy(src.at[low_rows], l_in.at[r, high_rows], l_send.at[r, 1], l_recv.at[r, 1], c + 1, s - 1),
            copy(src.at[high_rows], l_in.at[r, low_rows], l_send.at[r, 2], l_recv.at[r, 2], c + 1, s + 1),
        )

    def product_copy(k, r):
        partner = c + (1 << k) * (1 - 2 * ((c // (1 << k)) % 2))
        return copy(prods.at[k, r], others.at[k, r], k_send.at[k, r], k_recv.at[k, r], partner, s)

    @pl.when(above)
    def _():
        size_up().start()

    @pl.when(below)
    def _():
        size_down().start()

    @pl.when(c == cols - 1)
    def _():
        for r in range(row_count):
            r_out[r] = right_ref[r].reshape(2 * blk, width)
            r_in[r, mid_rows, :] = right_ref[r].reshape(2 * blk, width)
            _, down, up = right_copies(r, r_out.at[r], c)

            @pl.when(below)
            def _():
                down.start()

            @pl.when(above)
            def _():
                up.start()

    @pl.when(c == 0)
    def _():
        for r in range(row_count):
            l_in[r, low_rows, :] = jnp.zeros((blk, width), F32)
            l_in[r, mid_rows, :] = left_ref[r].reshape(2 * blk, width)
            l_in[r, high_rows, :] = jnp.zeros((blk, width), F32)

    for r in range(row_count):
        product_copy(0, r).start()

    first = lax.broadcasted_iota(jnp.int32, (blk, 2 * blk), 1) < blk
    zero = jnp.zeros((blk, 2 * blk), F32)
    for r in range(row_count):
        parts = [a_ref[r, 0, p] for p in range(3)]
        matrix = jnp.concatenate(
            [
                jnp.where(first, parts[0], zero),
                jnp.where(first, parts[1], parts[0]),
                jnp.where(first, parts[2], parts[1]),
                jnp.where(first, zero, parts[2]),
            ],
            axis=0,
        )
        a_wide[r] = wide(matrix)
        at_tall[r] = jnp.concatenate(split(matrix.T), axis=0)

    @pl.when(below)
    def _():
        size_up().wait_recv()

    @pl.when(above)
    def _():
        size_down().wait_recv()

    place = lax.broadcasted_iota(jnp.int32, (blk, width), 0).astype(F32)
    for b, limit in enumerate((halo_sizes[0:1, :], sizes[0:1, :], sizes[8:9, :], halo_sizes[8:9, :])):
        live = (place < limit).astype(F32)
        for r in range(row_count):
            weight[r, b * blk : (b + 1) * blk, :] = live * norms[r]

    def left_step():
        for r in range(row_count):
            main, down, up = left_copies(r)

            @pl.when(before)
            def _():
                main.wait_recv()

            @pl.when(before & above)
            def _():
                down.wait_recv()

            @pl.when(before & below)
            def _():
                up.wait_recv()

            env = jnp.concatenate(
                [
                    l_in[r, blk : 2 * blk, :] + l_in[r, 0:blk, :],
                    l_in[r, 2 * blk : 3 * blk, :] + l_in[r, 3 * blk : 4 * blk, :],
                ],
                axis=0,
            )
            m_keep[r] = env

            @pl.when(after)
            def _():
                l_out[r] = times(a_wide[r], env) * weight[r]
                main.start()

                @pl.when(below)
                def _():
                    down.start()

                @pl.when(above)
                def _():
                    up.start()

    def right_step():
        for r in range(row_count):
            main, down, up = right_copies(r, r_out.at[r], c - 1)

            @pl.when(after)
            def _():
                main.wait_recv()

            @pl.when(above)
            def _():
                down.wait_recv()

            @pl.when(below)
            def _():
                up.wait_recv()

            env = r_in[r] * weight[r]
            x_keep[r] = env

            @pl.when(before)
            def _():
                @pl.when((c == cols - 1) & below)
                def _():
                    down.wait_send()

                @pl.when((c == cols - 1) & above)
                def _():
                    up.wait_send()

                both = dot(at_tall[r], wide(env), ((1,), (0,)))
                half = both[: 2 * blk] + both[2 * blk :]
                r_out[r] = half[:, :width] + half[:, width:]
                main.start()

                @pl.when(below)
                def _():
                    down.start()

                @pl.when(above)
                def _():
                    up.start()

    def product_round(k):
        upper = (c // (1 << k)) % 2 == 1
        for r in range(row_count):
            product_copy(k, r).wait_recv()
            mine, other = prods[k, r], others[k, r]
            x = jnp.where(upper, other, mine)
            y = jnp.where(upper, mine, other)
            prods[k + 1, r] = times(wide(x), y)
            if k + 1 < rounds:
                product_copy(k + 1, r).start()

    early = c < cols // 2

    def fold():
        @pl.when(early)
        def _():
            for r in range(row_count):
                y_keep[r] = times(wide(m_keep[r]), prods[rounds, r])

        @pl.when(jnp.logical_not(early))
        def _():
            for r in range(row_count):
                x_keep[r] = times_t(wide(x_keep[r]), prods[rounds, r])

    def slot(t, carry):
        @pl.when(c == t)
        def _():
            left_step()

        @pl.when(c == cols - 1 - t)
        def _():
            right_step()

        for k in range(rounds):

            @pl.when(t == k)
            def _():
                product_round(k)

        @pl.when(t == cols - 2)
        def _():
            fold()

        return carry

    lax.fori_loop(0, cols, slot, 0)

    scale = 1.0 / math.sqrt(width)
    for r in range(row_count):

        @pl.when(jnp.logical_not(early))
        def _():
            y_keep[r] = m_keep[r]

        full = times_t(wide(x_keep[r]), y_keep[r]) * scale
        for p in range(3):
            out_ref[r, 0, p] = jnp.where(
                first, full[p * blk : (p + 1) * blk], full[(p + 1) * blk : (p + 2) * blk]
            )

    @pl.when(above)
    def _():
        size_up().wait_send()

    @pl.when(below)
    def _():
        size_down().wait_send()

    for r in range(row_count):
        for k in range(rounds):
            product_copy(k, r).wait_send()
        for there, (main, down, up) in (
            (after, left_copies(r)),
            (before, right_copies(r, r_out.at[r], c - 1)),
        ):

            @pl.when(there)
            def _():
                main.wait_send()

            @pl.when(there & below)
            def _():
                down.wait_send()

            @pl.when(there & above)
            def _():
                up.wait_send()


def body(cols, secs, couplings, lower_sites, left_edge, right_edge, bond_sizes):
    row_count, _, _, blk, lanes = couplings.shape
    width = lower_sites.shape[3]
    rounds = cols.bit_length() - 1
    dma = pltpu.SemaphoreType.DMA
    vmem = pl.BlockSpec(memory_space=pltpu.VMEM)
    return pl.pallas_call(
        functools.partial(kernel, cols, secs),
        out_shape=jax.ShapeDtypeStruct(couplings.shape, F32),
        in_specs=[vmem] * 4 + [pl.BlockSpec(memory_space=pltpu.SMEM)],
        out_specs=vmem,
        scratch_shapes=[
            pltpu.VMEM((row_count, 4 * blk, width), F32),
            pltpu.VMEM((row_count, 4 * blk, width), F32),
            pltpu.VMEM((row_count, 4 * blk, width), F32),
            pltpu.VMEM((row_count, 2 * blk, width), F32),
            pltpu.VMEM((row_count, 2 * blk, width), F32),
            pltpu.VMEM((row_count, 4 * blk, width), F32),
            pltpu.VMEM((row_count, 2 * blk, width), F32),
            pltpu.VMEM((row_count, 4 * blk, 2 * lanes), BF16),
            pltpu.VMEM((row_count, 2 * lanes, 4 * blk), BF16),
            pltpu.VMEM((row_count, 4 * blk, width), F32),
            pltpu.VMEM((16, width), F32),
            pltpu.VMEM((16, width), F32),
            pltpu.VMEM((rounds + 1, row_count, width, width), F32),
            pltpu.VMEM((rounds, row_count, width, width), F32),
            dma((row_count, 3)),
            dma((row_count, 3)),
            dma((row_count, 3)),
            dma((row_count, 3)),
            dma((2,)),
            dma((2,)),
            dma((rounds, row_count)),
            dma((rounds, row_count)),
        ],
        compiler_params=pltpu.CompilerParams(
            collective_id=0, has_side_effects=True, vmem_limit_bytes=32 * 1024 * 1024
        ),
    )(couplings, lower_sites, left_edge, right_edge, bond_sizes)


def solution(mesh):
    in_specs = (
        P(None, "col", None, None, "sec"),
        P(None, "col", None, None),
        P(None, "sec", None, None),
        P(None, "sec", None, None),
        P("col", "sec"),
    )
    out_specs = P(None, "col", None, None, "sec")
    run = functools.partial(body, mesh.shape["col"], mesh.shape["sec"])
    return jax.shard_map(run, mesh=mesh, in_specs=in_specs, out_specs=out_specs, check_vma=False)
```

```python
import functools
import math

import jax
import jax.numpy as jnp
from jax import lax
from jax.experimental import pallas as pl
from jax.experimental.pallas import tpu as pltpu
from jax.sharding import PartitionSpec as P

MESH = pl.DeviceIdType.MESH
F32 = jnp.float32
BF16 = jnp.bfloat16


def split(x):
    high = x.astype(BF16)
    low = (x - high.astype(F32)).astype(BF16)
    return high, low


def wide(x):
    return jnp.concatenate(split(x), axis=1)


def dot(a, b, contract):
    return lax.dot_general(a, b, (contract, ((), ())), preferred_element_type=F32)


def times(x_wide, y):
    pair = wide(y)
    both = dot(x_wide, jnp.concatenate([pair, pair], axis=0), ((1,), (0,)))
    n = y.shape[1]
    return both[:, :n] + both[:, n:]


def times_t(x_wide, y):
    high, low = split(y)
    rows = jnp.concatenate(
        [jnp.concatenate([high, high], axis=1), jnp.concatenate([low, low], axis=1)], axis=0
    )
    both = dot(x_wide, rows, ((1,), (1,)))
    n = y.shape[0]
    return both[:, :n] + both[:, n:]


def kernel(
    cols, secs, a_hbm, b_hbm, left_hbm, right_hbm, size_hbm, out_ref, a_ref, b_ref, size_ref,
    l_in, r_in, l_out, r_out, m_keep, x_keep, y_keep, a_wide, at_tall, weight, sizes, halo_sizes, prods, others,
    l_send, l_recv, r_send, r_recv, h_send, h_recv, k_send, k_recv, local,
):
    row_count = a_ref.shape[0]
    blk = a_ref.shape[3]
    width = b_ref.shape[3]
    rounds = cols.bit_length() - 1
    c = lax.axis_index("col")
    s = lax.axis_index("sec")
    below, above = s > 0, s < secs - 1
    before, after = c > 0, c < cols - 1
    low_rows, mid_rows, high_rows = pl.ds(0, blk), pl.ds(blk, 2 * blk), pl.ds(3 * blk, blk)

    def copy(src, dst, send, recv, dc, ds):
        return pltpu.make_async_remote_copy(
            src_ref=src, dst_ref=dst, send_sem=send, recv_sem=recv,
            device_id=(dc, ds), device_id_type=MESH,
        )

    load_a = pltpu.make_async_copy(a_hbm, a_ref, local.at[0])
    load_b = pltpu.make_async_copy(b_hbm, b_ref, local.at[1])
    load_size = pltpu.make_async_copy(size_hbm, size_ref, local.at[2])
    load_left = pltpu.make_async_copy(left_hbm, l_in.at[:, mid_rows], local.at[3])
    load_right = pltpu.make_async_copy(right_hbm, r_out, local.at[4])
    load_size.start()
    load_b.start()
    load_a.start()

    @pl.when(c == 0)
    def _():
        load_left.start()

    @pl.when(c == cols - 1)
    def _():
        load_right.start()

    barrier = pltpu.get_barrier_semaphore()
    count = jnp.int32(rounds)
    for k in range(rounds):
        partner = c + (1 << k) * (1 - 2 * ((c // (1 << k)) % 2))
        pl.semaphore_signal(barrier, inc=1, device_id=(partner, s), device_id_type=MESH)
    for dc, there in ((0, None), (-1, before), (1, after)):
        for ds, beside in ((0, None), (-1, below), (1, above)):
            if dc == 0 and ds == 0:
                continue
            if there is None:
                exists = beside
            elif beside is None:
                exists = there
            else:
                exists = there & beside
            count = count + exists.astype(jnp.int32)

            @pl.when(exists)
            def _(dc=dc, ds=ds):
                pl.semaphore_signal(barrier, inc=1, device_id=(c + dc, s + ds), device_id_type=MESH)

    load_size.wait()
    sizes[0:8, :] = jnp.full((8, width), size_ref[0, 0].astype(F32), F32)
    sizes[8:16, :] = jnp.full((8, width), size_ref[0, 1].astype(F32), F32)
    norms = []
    load_b.wait()
    for r in range(row_count):
        lower = b_ref[r, 0]
        norm = jnp.max(jnp.sum(jnp.abs(lower), axis=1, keepdims=True), axis=0, keepdims=True)
        norm = jnp.maximum(norm, 1e-30)
        norms.append(norm)
        prods[0, r] = lower / norm

    @pl.when(s == 0)
    def _():
        halo_sizes[0:8, :] = jnp.zeros((8, width), F32)
        r_in[:, low_rows, :] = jnp.zeros((row_count, blk, width), F32)
        l_in[:, low_rows, :] = jnp.zeros((row_count, blk, width), F32)

    @pl.when(s == secs - 1)
    def _():
        halo_sizes[8:16, :] = jnp.zeros((8, width), F32)
        r_in[:, high_rows, :] = jnp.zeros((row_count, blk, width), F32)
        l_in[:, high_rows, :] = jnp.zeros((row_count, blk, width), F32)

    pl.semaphore_wait(barrier, count)

    def size_up():
        return copy(sizes.at[8:16], halo_sizes.at[0:8], h_send.at[0], h_recv.at[0], c, s + 1)

    def size_down():
        return copy(sizes.at[0:8], halo_sizes.at[8:16], h_send.at[1], h_recv.at[1], c, s - 1)

    def right_copies(r, src, dc):
        return (
            copy(src.at[pl.ds(0, 2 * blk)], r_in.at[r, mid_rows], r_send.at[r, 0], r_recv.at[r, 0], dc, s),
            copy(src.at[pl.ds(0, blk)], r_in.at[r, high_rows], r_send.at[r, 1], r_recv.at[r, 1], dc, s - 1),
            copy(src.at[pl.ds(blk, blk)], r_in.at[r, low_rows], r_send.at[r, 2], r_recv.at[r, 2], dc, s + 1),
        )

    def left_copies(r):
        src = l_out.at[r]
        return (
            copy(src.at[mid_rows], l_in.at[r, mid_rows], l_send.at[r, 0], l_recv.at[r, 0], c + 1, s),
            copy(src.at[low_rows], l_in.at[r, high_rows], l_send.at[r, 1], l_recv.at[r, 1], c + 1, s - 1),
            copy(src.at[high_rows], l_in.at[r, low_rows], l_send.at[r, 2], l_recv.at[r, 2], c + 1, s + 1),
        )

    def product_copy(k, r):
        partner = c + (1 << k) * (1 - 2 * ((c // (1 << k)) % 2))
        return copy(prods.at[k, r], others.at[k, r], k_send.at[k, r], k_recv.at[k, r], partner, s)

    @pl.when(above)
    def _():
        size_up().start()

    @pl.when(below)
    def _():
        size_down().start()

    @pl.when(c == cols - 1)
    def _():
        load_right.wait()
        for r in range(row_count):
            r_in[r, mid_rows, :] = r_out[r]
            _, down, up = right_copies(r, r_out.at[r], c)

            @pl.when(below)
            def _():
                down.start()

            @pl.when(above)
            def _():
                up.start()

    @pl.when(c == 0)
    def _():
        for r in range(row_count):
            l_in[r, low_rows, :] = jnp.zeros((blk, width), F32)
            l_in[r, high_rows, :] = jnp.zeros((blk, width), F32)
        load_left.wait()

    for r in range(row_count):
        product_copy(0, r).start()

    first = lax.broadcasted_iota(jnp.int32, (blk, 2 * blk), 1) < blk
    zero = jnp.zeros((blk, 2 * blk), F32)
    load_a.wait()
    for r in range(row_count):
        parts = [a_ref[r, 0, p] for p in range(3)]
        matrix = jnp.concatenate(
            [
                jnp.where(first, parts[0], zero),
                jnp.where(first, parts[1], parts[0]),
                jnp.where(first, parts[2], parts[1]),
                jnp.where(first, zero, parts[2]),
            ],
            axis=0,
        )
        a_wide[r] = wide(matrix)
        at_tall[r] = jnp.concatenate(split(matrix.T), axis=0)

    @pl.when(below)
    def _():
        size_up().wait_recv()

    @pl.when(above)
    def _():
        size_down().wait_recv()

    place = lax.broadcasted_iota(jnp.int32, (blk, width), 0).astype(F32)
    for b, limit in enumerate((halo_sizes[0:1, :], sizes[0:1, :], sizes[8:9, :], halo_sizes[8:9, :])):
        live = (place < limit).astype(F32)
        for r in range(row_count):
            weight[r, b * blk : (b + 1) * blk, :] = live * norms[r]

    def left_step():
        for r in range(row_count):
            main, down, up = left_copies(r)

            @pl.when(before)
            def _():
                main.wait_recv()

            @pl.when(before & above)
            def _():
                down.wait_recv()

            @pl.when(before & below)
            def _():
                up.wait_recv()

            env = jnp.concatenate(
                [
                    l_in[r, blk : 2 * blk, :] + l_in[r, 0:blk, :],
                    l_in[r, 2 * blk : 3 * blk, :] + l_in[r, 3 * blk : 4 * blk, :],
                ],
                axis=0,
            )
            m_keep[r] = env

            @pl.when(after)
            def _():
                l_out[r] = times(a_wide[r], env) * weight[r]
                main.start()

                @pl.when(below)
                def _():
                    down.start()

                @pl.when(above)
                def _():
                    up.start()

    def right_step():
        for r in range(row_count):
            main, down, up = right_copies(r, r_out.at[r], c - 1)

            @pl.when(after)
            def _():
                main.wait_recv()

            @pl.when(above)
            def _():
                down.wait_recv()

            @pl.when(below)
            def _():
                up.wait_recv()

            env = r_in[r] * weight[r]
            x_keep[r] = env

            @pl.when(before)
            def _():
                @pl.when((c == cols - 1) & below)
                def _():
                    down.wait_send()

                @pl.when((c == cols - 1) & above)
                def _():
                    up.wait_send()

                both = dot(at_tall[r], wide(env), ((1,), (0,)))
                half = both[: 2 * blk] + both[2 * blk :]
                r_out[r] = half[:, :width] + half[:, width:]
                main.start()

                @pl.when(below)
                def _():
                    down.start()

                @pl.when(above)
                def _():
                    up.start()

    def product_round(k):
        upper = (c // (1 << k)) % 2 == 1
        for r in range(row_count):
            product_copy(k, r).wait_recv()
            mine, other = prods[k, r], others[k, r]
            x = jnp.where(upper, other, mine)
            y = jnp.where(upper, mine, other)
            prods[k + 1, r] = times(wide(x), y)
            if k + 1 < rounds:
                product_copy(k + 1, r).start()

    early = c < cols // 2

    def fold():
        @pl.when(early)
        def _():
            for r in range(row_count):
                y_keep[r] = times(wide(m_keep[r]), prods[rounds, r])

        @pl.when(jnp.logical_not(early))
        def _():
            for r in range(row_count):
                x_keep[r] = times_t(wide(x_keep[r]), prods[rounds, r])

    def slot(t, carry):
        @pl.when(c == t)
        def _():
            left_step()

        @pl.when(c == cols - 1 - t)
        def _():
            right_step()

        for k in range(rounds):

            @pl.when(t == k)
            def _():
                product_round(k)

        @pl.when(t == cols - 2)
        def _():
            fold()

        return carry

    lax.fori_loop(0, cols, slot, 0)

    scale = 1.0 / math.sqrt(width)
    for r in range(row_count):

        @pl.when(jnp.logical_not(early))
        def _():
            y_keep[r] = m_keep[r]

        full = times_t(wide(x_keep[r]), y_keep[r]) * scale
        for p in range(3):
            out_ref[r, 0, p] = jnp.where(
                first, full[p * blk : (p + 1) * blk], full[(p + 1) * blk : (p + 2) * blk]
            )

    @pl.when(above)
    def _():
        size_up().wait_send()

    @pl.when(below)
    def _():
        size_down().wait_send()

    for r in range(row_count):
        for k in range(rounds):
            product_copy(k, r).wait_send()
        for there, (main, down, up) in (
            (after, left_copies(r)),
            (before, right_copies(r, r_out.at[r], c - 1)),
        ):

            @pl.when(there)
            def _():
                main.wait_send()

            @pl.when(there & below)
            def _():
                down.wait_send()

            @pl.when(there & above)
            def _():
                up.wait_send()


def body(cols, secs, couplings, lower_sites, left_edge, right_edge, bond_sizes):
    row_count, _, _, blk, lanes = couplings.shape
    width = lower_sites.shape[3]
    rounds = cols.bit_length() - 1
    dma = pltpu.SemaphoreType.DMA
    left_edge = left_edge.reshape(row_count, lanes, width)
    right_edge = right_edge.reshape(row_count, lanes, width)
    vmem = pl.BlockSpec(memory_space=pltpu.VMEM)
    return pl.pallas_call(
        functools.partial(kernel, cols, secs),
        out_shape=jax.ShapeDtypeStruct(couplings.shape, F32),
        in_specs=[pl.BlockSpec(memory_space=pltpu.HBM)] * 5,
        out_specs=vmem,
        scratch_shapes=[
            pltpu.VMEM(couplings.shape, F32),
            pltpu.VMEM(lower_sites.shape, F32),
            pltpu.SMEM(bond_sizes.shape, jnp.int32),
            pltpu.VMEM((row_count, 4 * blk, width), F32),
            pltpu.VMEM((row_count, 4 * blk, width), F32),
            pltpu.VMEM((row_count, 4 * blk, width), F32),
            pltpu.VMEM((row_count, 2 * blk, width), F32),
            pltpu.VMEM((row_count, 2 * blk, width), F32),
            pltpu.VMEM((row_count, 4 * blk, width), F32),
            pltpu.VMEM((row_count, 2 * blk, width), F32),
            pltpu.VMEM((row_count, 4 * blk, 2 * lanes), BF16),
            pltpu.VMEM((row_count, 2 * lanes, 4 * blk), BF16),
            pltpu.VMEM((row_count, 4 * blk, width), F32),
            pltpu.VMEM((16, width), F32),
            pltpu.VMEM((16, width), F32),
            pltpu.VMEM((rounds + 1, row_count, width, width), F32),
            pltpu.VMEM((rounds, row_count, width, width), F32),
            dma((row_count, 3)),
            dma((row_count, 3)),
            dma((row_count, 3)),
            dma((row_count, 3)),
            dma((2,)),
            dma((2,)),
            dma((rounds, row_count)),
            dma((rounds, row_count)),
            dma((5,)),
        ],
        compiler_params=pltpu.CompilerParams(
            collective_id=0, has_side_effects=True, vmem_limit_bytes=64 * 1024 * 1024 - 65536
        ),
    )(couplings, lower_sites, left_edge, right_edge, bond_sizes)


def solution(mesh):
    in_specs = (
        P(None, "col", None, None, "sec"),
        P(None, "col", None, None),
        P(None, "sec", None, None),
        P(None, "sec", None, None),
        P("col", "sec"),
    )
    out_specs = P(None, "col", None, None, "sec")
    run = functools.partial(body, mesh.shape["col"], mesh.shape["sec"])
    return jax.shard_map(run, mesh=mesh, in_specs=in_specs, out_specs=out_specs, check_vma=False)
```

```python
import functools
import math

import jax
import jax.numpy as jnp
from jax import lax
from jax.experimental import pallas as pl
from jax.experimental.pallas import tpu as pltpu
from jax.sharding import PartitionSpec as P

MESH = pl.DeviceIdType.MESH
F32 = jnp.float32
BF16 = jnp.bfloat16


def split(x):
    high = x.astype(BF16)
    low = (x - high.astype(F32)).astype(BF16)
    return high, low


def wide(x):
    return jnp.concatenate(split(x), axis=1)


def dot(a, b, contract):
    return lax.dot_general(a, b, (contract, ((), ())), preferred_element_type=F32)


def times(x_wide, y):
    pair = wide(y)
    both = dot(x_wide, jnp.concatenate([pair, pair], axis=0), ((1,), (0,)))
    n = y.shape[1]
    return both[:, :n] + both[:, n:]


def times_t(x_wide, y):
    high, low = split(y)
    rows = jnp.concatenate(
        [jnp.concatenate([high, high], axis=1), jnp.concatenate([low, low], axis=1)], axis=0
    )
    both = dot(x_wide, rows, ((1,), (1,)))
    n = y.shape[0]
    return both[:, :n] + both[:, n:]


def kernel(
    cols, secs, a_hbm, b_hbm, left_hbm, right_hbm, size_hbm, out_ref, a_ref, b_ref, size_ref,
    l_in, r_in, l_out, r_out, m_keep, x_keep, y_keep, a_wide, at_tall, weight, sizes, halo_sizes, halo_a, prods, others,
    l_send, l_recv, r_send, r_recv, h_send, h_recv, a_send, a_recv, k_send, k_recv, local,
):
    row_count = a_ref.shape[0]
    blk = a_ref.shape[3]
    width = b_ref.shape[3]
    rounds = cols.bit_length() - 1
    c = lax.axis_index("col")
    s = lax.axis_index("sec")
    below, above = s > 0, s < secs - 1
    before, after = c > 0, c < cols - 1
    odd = c % 2 == 1
    even = jnp.logical_not(odd)
    low_rows, mid_rows, high_rows = pl.ds(0, 2 * blk), pl.ds(2 * blk, 2 * blk), pl.ds(4 * blk, 2 * blk)
    near_rows = pl.ds(blk, 4 * blk)

    def copy(src, dst, send, recv, dc, ds):
        return pltpu.make_async_remote_copy(
            src_ref=src, dst_ref=dst, send_sem=send, recv_sem=recv,
            device_id=(dc, ds), device_id_type=MESH,
        )

    load_a = pltpu.make_async_copy(a_hbm, a_ref, local.at[0])
    load_b = pltpu.make_async_copy(b_hbm, b_ref, local.at[1])
    load_size = pltpu.make_async_copy(size_hbm, size_ref, local.at[2])
    load_left = pltpu.make_async_copy(left_hbm, l_in.at[:, mid_rows], local.at[3])
    load_right = pltpu.make_async_copy(right_hbm, r_in.at[:, mid_rows], local.at[4])
    load_size.start()
    load_b.start()
    load_a.start()

    @pl.when(c == 0)
    def _():
        load_left.start()

    @pl.when(c == cols - 1)
    def _():
        load_right.start()

    barrier = pltpu.get_barrier_semaphore()
    count = jnp.int32(rounds)
    for k in range(rounds):
        partner = c + (1 << k) * (1 - 2 * ((c // (1 << k)) % 2))
        pl.semaphore_signal(barrier, inc=1, device_id=(partner, s), device_id_type=MESH)
    for dc, there in ((0, None), (-1, before), (1, after)):
        for ds, beside in ((0, None), (-1, below), (1, above)):
            if dc == 0 and ds == 0:
                continue
            if there is None:
                exists = beside
            elif beside is None:
                exists = there
            else:
                exists = there & beside
            count = count + exists.astype(jnp.int32)

            @pl.when(exists)
            def _(dc=dc, ds=ds):
                pl.semaphore_signal(barrier, inc=1, device_id=(c + dc, s + ds), device_id_type=MESH)

    load_size.wait()
    sizes[0:8, :] = jnp.full((8, width), size_ref[0, 0].astype(F32), F32)
    sizes[8:16, :] = jnp.full((8, width), size_ref[0, 1].astype(F32), F32)
    norms = []
    load_b.wait()
    for r in range(row_count):
        lower = b_ref[r, 0]
        norm = jnp.max(jnp.sum(jnp.abs(lower), axis=1, keepdims=True), axis=0, keepdims=True)
        norm = jnp.maximum(norm, 1e-30)
        norms.append(norm)
        prods[0, r] = lower / norm

    def clear(ref, start, length):
        for r in range(row_count):
            ref[r, start : start + length, :] = jnp.zeros((length, width), F32)

    @pl.when(s == 0)
    def _():
        halo_sizes[0] = jnp.zeros((16, width), F32)
        halo_a[0] = jnp.zeros(halo_a.shape[1:], F32)

    @pl.when(s == secs - 1)
    def _():
        halo_sizes[1] = jnp.zeros((16, width), F32)
        halo_a[1] = jnp.zeros(halo_a.shape[1:], F32)

    for near, ref in ((odd, l_in), (even, r_in)):

        @pl.when(near)
        def _(ref=ref):
            clear(ref, 0, blk)
            clear(ref, 5 * blk, blk)

        @pl.when(jnp.logical_not(near) & (s == 0))
        def _(ref=ref):
            clear(ref, 0, 2 * blk)

        @pl.when(jnp.logical_not(near) & (s == secs - 1))
        def _(ref=ref):
            clear(ref, 4 * blk, 2 * blk)

    pl.semaphore_wait(barrier, count)

    def halo_copies(side, to):
        return [copy(sizes, halo_sizes.at[side], h_send.at[side], h_recv.at[side], c, to)] + [
            copy(a_ref.at[r], halo_a.at[side, r], a_send.at[side, r], a_recv.at[side, r], c, to)
            for r in range(row_count)
        ]

    def far_copies(src, dst, send, recv, to):
        return (
            copy(src, dst.at[mid_rows], send.at[0], recv.at[0], to, s),
            copy(src, dst.at[high_rows], send.at[1], recv.at[1], to, s - 1),
            copy(src, dst.at[low_rows], send.at[2], recv.at[2], to, s + 1),
        )

    def near_copy(src, dst, send, recv, to):
        return copy(src, dst.at[near_rows], send.at[0], recv.at[0], to, s)

    class Way:
        def __init__(self, src, dst, send, recv, to):
            self.args = (src, dst, send, recv)
            self.to = to

        def far(self, r, to=None, src=None):
            own, dst, send, recv = (ref.at[r] for ref in self.args)
            src = own.at[pl.ds(blk, 2 * blk)] if src is None else src
            return far_copies(src, dst, send, recv, self.to if to is None else to)

        def near(self, r):
            src, dst, send, recv = (ref.at[r] for ref in self.args)
            return near_copy(src, dst, send, recv, self.to)

    left = Way(l_out, l_in, l_send, l_recv, c + 1)
    right = Way(r_out, r_in, r_send, r_recv, c - 1)

    def edge_copies(way, r):
        return way.far(r, c, way.args[1].at[r, mid_rows])

    def sideways(copies, act, here=None):
        _, down, up = copies
        for exists, one in ((below, down), (above, up)):

            @pl.when(exists if here is None else exists & here)
            def _(one=one):
                act(one)

    def product_copy(k, r):
        partner = c + (1 << k) * (1 - 2 * ((c // (1 << k)) % 2))
        return copy(prods.at[k, r], others.at[k, r], k_send.at[k, r], k_recv.at[k, r], partner, s)

    load_a.wait()

    for exists, side, to in ((above, 0, s + 1), (below, 1, s - 1)):

        @pl.when(exists)
        def _(side=side, to=to):
            for one in halo_copies(side, to):
                one.start()

    for here, load, way in ((c == 0, load_left, left), (c == cols - 1, load_right, right)):

        @pl.when(here)
        def _(load=load, way=way):
            load.wait()
            for r in range(row_count):
                sideways(edge_copies(way, r), lambda one: one.start())

    for r in range(row_count):
        product_copy(0, r).start()

    first = lax.broadcasted_iota(jnp.int32, (blk, 2 * blk), 1) < blk
    zero = jnp.zeros((blk, 2 * blk), F32)

    def spread(of_first, of_second, height):
        return jnp.concatenate([jnp.where(first, of_first(n), of_second(n)) for n in range(height)], axis=0)

    for exists, side, to in ((below, 0, s - 1), (above, 1, s + 1)):

        @pl.when(exists)
        def _(side=side, to=to):
            for one in halo_copies(side, to):
                one.wait_recv()

    place = lax.broadcasted_iota(jnp.int32, (blk, width), 0).astype(F32)
    limits = [sizes[0:1, :], sizes[8:9, :]]
    limits = [halo_sizes[0, 0:1, :], halo_sizes[0, 8:9, :]] + limits
    limits = limits + [halo_sizes[1, 0:1, :], halo_sizes[1, 8:9, :]]
    for b, limit in enumerate(limits):
        live = (place < limit).astype(F32)
        for r in range(row_count):
            weight[r, b * blk : (b + 1) * blk, :] = live * norms[r]

    for r in range(row_count):

        def part(ref):
            return lambda p: ref[p] if 0 <= p <= 2 else zero

        low, own, high = part(halo_a.at[0, r, 0]), part(a_ref.at[r, 0]), part(halo_a.at[1, r, 0])
        groups = [
            spread(lambda n, g=g, one=one: one(n - 2 * g + 2), lambda n, g=g, one=one: one(n - 2 * g + 1), 4)
            for g, one in enumerate((low, own, high))
        ]
        a_wide[r] = wide(jnp.concatenate(groups, axis=1))
        inner = spread(lambda n: own(n - 1), lambda n: own(n - 2), 6)
        outer = spread(lambda n: high(n - 3), lambda n: low(n), 6)
        at_tall[r] = jnp.concatenate(split(jnp.concatenate([inner.T, outer.T], axis=0)), axis=0)

    def receive(way, r, near, start):
        @pl.when(near)
        def _():
            way.near(r).wait_recv()

        @pl.when(jnp.logical_not(near))
        def _():
            main, down, up = way.far(r)

            @pl.when(jnp.logical_not(start))
            def _():
                main.wait_recv()

            sideways((main, up, down), lambda one: one.wait_recv())

    def send(way, r, near):
        @pl.when(near)
        def _():
            way.near(r).start()

        @pl.when(jnp.logical_not(near))
        def _():
            copies = way.far(r)
            sideways(copies, lambda one: one.start())
            copies[0].start()

    def left_step():
        for r in range(row_count):
            receive(left, r, odd, c == 0)
            m_keep[r] = l_in[r, mid_rows, :]

            @pl.when(after)
            def _(r=r):
                l_out[r] = times(a_wide[r], l_in[r]) * weight[r, near_rows, :]
                send(left, r, even)

    def right_step():
        for r in range(row_count):
            receive(right, r, even, c == cols - 1)
            x_keep[r] = r_in[r, near_rows, :] * weight[r, near_rows, :]

            @pl.when(before)
            def _(r=r):
                both = dot(at_tall[r], wide(r_in[r] * weight[r]), ((1,), (0,)))
                half = both[: 4 * blk] + both[4 * blk :]
                half = half[:, :width] + half[:, width:]
                r_out[r, 0:blk, :] = half[3 * blk : 4 * blk]
                r_out[r, blk : 3 * blk, :] = half[0 : 2 * blk]
                r_out[r, 3 * blk : 4 * blk, :] = half[2 * blk : 3 * blk]
                send(right, r, odd)

    def product_round(k):
        upper = (c // (1 << k)) % 2 == 1
        for r in range(row_count):
            product_copy(k, r).wait_recv()
            mine, other = prods[k, r], others[k, r]
            x = jnp.where(upper, other, mine)
            y = jnp.where(upper, mine, other)
            prods[k + 1, r] = times(wide(x), y)
            if k + 1 < rounds:
                product_copy(k + 1, r).start()

    early = c < cols // 2

    def fold():
        @pl.when(early)
        def _():
            for r in range(row_count):
                y_keep[r] = times(wide(m_keep[r]), prods[rounds, r])

        @pl.when(jnp.logical_not(early))
        def _():
            for r in range(row_count):
                x_keep[r] = times_t(wide(x_keep[r]), prods[rounds, r])

    def slot(t, carry):
        @pl.when(c == t)
        def _():
            left_step()

        @pl.when(c == cols - 1 - t)
        def _():
            right_step()

        for k in range(rounds):

            @pl.when(t == 2 + 2 * k)
            def _():
                product_round(k)

        @pl.when(t == cols - 2)
        def _():
            fold()

        return carry

    lax.fori_loop(0, cols, slot, 0)

    scale = 1.0 / math.sqrt(width)
    for r in range(row_count):

        @pl.when(jnp.logical_not(early))
        def _():
            y_keep[r] = m_keep[r]

        full = times_t(wide(x_keep[r]), y_keep[r]) * scale
        for p in range(3):
            out_ref[r, 0, p] = jnp.where(
                first, full[p * blk : (p + 1) * blk], full[(p + 1) * blk : (p + 2) * blk]
            )

    for exists, side, to in ((above, 0, s + 1), (below, 1, s - 1)):

        @pl.when(exists)
        def _(side=side, to=to):
            for one in halo_copies(side, to):
                one.wait_send()

    for r in range(row_count):
        for k in range(rounds):
            product_copy(k, r).wait_send()
        for way, near, start, there in ((left, even, c == 0, after), (right, odd, c == cols - 1, before)):

            @pl.when(near & there)
            def _(way=way):
                way.near(r).wait_send()

            @pl.when(start)
            def _(way=way):
                sideways(edge_copies(way, r), lambda one: one.wait_send())

            @pl.when(jnp.logical_not(near) & there)
            def _(way=way):
                copies = way.far(r)
                copies[0].wait_send()
                sideways(copies, lambda one: one.wait_send())


def body(cols, secs, couplings, lower_sites, left_edge, right_edge, bond_sizes):
    row_count, _, _, blk, lanes = couplings.shape
    width = lower_sites.shape[3]
    rounds = cols.bit_length() - 1
    dma = pltpu.SemaphoreType.DMA
    left_edge = left_edge.reshape(row_count, lanes, width)
    right_edge = right_edge.reshape(row_count, lanes, width)
    vmem = pl.BlockSpec(memory_space=pltpu.VMEM)
    return pl.pallas_call(
        functools.partial(kernel, cols, secs),
        out_shape=jax.ShapeDtypeStruct(couplings.shape, F32),
        in_specs=[pl.BlockSpec(memory_space=pltpu.HBM)] * 5,
        out_specs=vmem,
        scratch_shapes=[
            pltpu.VMEM(couplings.shape, F32),
            pltpu.VMEM(lower_sites.shape, F32),
            pltpu.SMEM(bond_sizes.shape, jnp.int32),
            pltpu.VMEM((row_count, 6 * blk, width), F32),
            pltpu.VMEM((row_count, 6 * blk, width), F32),
            pltpu.VMEM((row_count, 4 * blk, width), F32),
            pltpu.VMEM((row_count, 4 * blk, width), F32),
            pltpu.VMEM((row_count, 2 * blk, width), F32),
            pltpu.VMEM((row_count, 4 * blk, width), F32),
            pltpu.VMEM((row_count, 2 * blk, width), F32),
            pltpu.VMEM((row_count, 4 * blk, 6 * lanes), BF16),
            pltpu.VMEM((row_count, 4 * lanes, 6 * blk), BF16),
            pltpu.VMEM((row_count, 6 * blk, width), F32),
            pltpu.VMEM((16, width), F32),
            pltpu.VMEM((2, 16, width), F32),
            pltpu.VMEM((2,) + couplings.shape, F32),
            pltpu.VMEM((rounds + 1, row_count, width, width), F32),
            pltpu.VMEM((rounds, row_count, width, width), F32),
            dma((row_count, 3)),
            dma((row_count, 3)),
            dma((row_count, 3)),
            dma((row_count, 3)),
            dma((2,)),
            dma((2,)),
            dma((2, row_count)),
            dma((2, row_count)),
            dma((rounds, row_count)),
            dma((rounds, row_count)),
            dma((5,)),
        ],
        compiler_params=pltpu.CompilerParams(
            collective_id=0, has_side_effects=True, vmem_limit_bytes=64 * 1024 * 1024 - 65536
        ),
    )(couplings, lower_sites, left_edge, right_edge, bond_sizes)


def solution(mesh):
    in_specs = (
        P(None, "col", None, None, "sec"),
        P(None, "col", None, None),
        P(None, "sec", None, None),
        P(None, "sec", None, None),
        P("col", "sec"),
    )
    out_specs = P(None, "col", None, None, "sec")
    run = functools.partial(body, mesh.shape["col"], mesh.shape["sec"])
    return jax.shard_map(run, mesh=mesh, in_specs=in_specs, out_specs=out_specs, check_vma=False)
```

```python
import functools
import math

import jax
import jax.numpy as jnp
from jax import lax
from jax.experimental import pallas as pl
from jax.experimental.pallas import tpu as pltpu
from jax.sharding import PartitionSpec as P

MESH = pl.DeviceIdType.MESH
F32 = jnp.float32
BF16 = jnp.bfloat16


def split(x):
    high = x.astype(BF16)
    low = (x - high.astype(F32)).astype(BF16)
    return high, low


def wide(x):
    return jnp.concatenate(split(x), axis=1)


def dot(a, b, contract):
    return lax.dot_general(a, b, (contract, ((), ())), preferred_element_type=F32)


def times(x_wide, y):
    pair = wide(y)
    both = dot(x_wide, jnp.concatenate([pair, pair], axis=0), ((1,), (0,)))
    n = y.shape[1]
    return both[:, :n] + both[:, n:]


def times_t(x_wide, y):
    high, low = split(y)
    rows = jnp.concatenate(
        [jnp.concatenate([high, high], axis=1), jnp.concatenate([low, low], axis=1)], axis=0
    )
    both = dot(x_wide, rows, ((1,), (1,)))
    n = y.shape[0]
    return both[:, :n] + both[:, n:]


def kernel(
    cols, secs, a_hbm, b_hbm, left_hbm, right_hbm, size_hbm, out_ref, a_ref, b_ref, size_ref,
    l_in, r_in, l_out, r_out, m_keep, x_keep, y_keep, a_wide, at_tall, weight, sizes, halo_sizes, prods, others,
    l_send, l_recv, r_send, r_recv, h_send, h_recv, k_send, k_recv, local,
):
    row_count = a_ref.shape[0]
    blk = a_ref.shape[3]
    width = b_ref.shape[3]
    rounds = cols.bit_length() - 1
    c = lax.axis_index("col")
    s = lax.axis_index("sec")
    below, above = s > 0, s < secs - 1
    before, after = c > 0, c < cols - 1
    low_rows, mid_rows, high_rows = pl.ds(0, blk), pl.ds(blk, 2 * blk), pl.ds(3 * blk, blk)

    def copy(src, dst, send, recv, dc, ds):
        return pltpu.make_async_remote_copy(
            src_ref=src, dst_ref=dst, send_sem=send, recv_sem=recv,
            device_id=(dc, ds), device_id_type=MESH,
        )

    load_a = pltpu.make_async_copy(a_hbm, a_ref, local.at[0])
    load_b = pltpu.make_async_copy(b_hbm, b_ref, local.at[1])
    load_size = pltpu.make_async_copy(size_hbm, size_ref, local.at[2])
    load_left = pltpu.make_async_copy(left_hbm, l_in.at[:, mid_rows], local.at[3])
    load_right = pltpu.make_async_copy(right_hbm, r_out, local.at[4])
    load_size.start()
    load_b.start()
    load_a.start()

    @pl.when(c == 0)
    def _():
        load_left.start()

    @pl.when(c == cols - 1)
    def _():
        load_right.start()

    barrier = pltpu.get_barrier_semaphore()
    count = jnp.int32(rounds)
    for k in range(rounds):
        partner = c + (1 << k) * (1 - 2 * ((c // (1 << k)) % 2))
        pl.semaphore_signal(barrier, inc=1, device_id=(partner, s), device_id_type=MESH)
    for dc, there in ((0, None), (-1, before), (1, after)):
        for ds, beside in ((0, None), (-1, below), (1, above)):
            if dc == 0 and ds == 0:
                continue
            if there is None:
                exists = beside
            elif beside is None:
                exists = there
            else:
                exists = there & beside
            count = count + exists.astype(jnp.int32)

            @pl.when(exists)
            def _(dc=dc, ds=ds):
                pl.semaphore_signal(barrier, inc=1, device_id=(c + dc, s + ds), device_id_type=MESH)

    load_size.wait()
    sizes[0:8, :] = jnp.full((8, width), size_ref[0, 0].astype(F32), F32)
    sizes[8:16, :] = jnp.full((8, width), size_ref[0, 1].astype(F32), F32)
    norms = []
    load_b.wait()
    for r in range(row_count):
        lower = b_ref[r, 0]
        norm = jnp.max(jnp.sum(jnp.abs(lower), axis=1, keepdims=True), axis=0, keepdims=True)
        norm = jnp.maximum(norm, 1e-30)
        norms.append(norm)
        prods[0, r] = lower / norm

    @pl.when(s == 0)
    def _():
        halo_sizes[0:8, :] = jnp.zeros((8, width), F32)
        r_in[:, low_rows, :] = jnp.zeros((row_count, blk, width), F32)
        l_in[:, low_rows, :] = jnp.zeros((row_count, blk, width), F32)

    @pl.when(s == secs - 1)
    def _():
        halo_sizes[8:16, :] = jnp.zeros((8, width), F32)
        r_in[:, high_rows, :] = jnp.zeros((row_count, blk, width), F32)
        l_in[:, high_rows, :] = jnp.zeros((row_count, blk, width), F32)

    pl.semaphore_wait(barrier, count)

    def size_up():
        return copy(sizes.at[8:16], halo_sizes.at[0:8], h_send.at[0], h_recv.at[0], c, s + 1)

    def size_down():
        return copy(sizes.at[0:8], halo_sizes.at[8:16], h_send.at[1], h_recv.at[1], c, s - 1)

    def right_copies(r, src, dc):
        return (
            copy(src.at[pl.ds(0, 2 * blk)], r_in.at[r, mid_rows], r_send.at[r, 0], r_recv.at[r, 0], dc, s),
            copy(src.at[pl.ds(0, blk)], r_in.at[r, high_rows], r_send.at[r, 1], r_recv.at[r, 1], dc, s - 1),
            copy(src.at[pl.ds(blk, blk)], r_in.at[r, low_rows], r_send.at[r, 2], r_recv.at[r, 2], dc, s + 1),
        )

    def left_copies(r):
        src = l_out.at[r]
        return (
            copy(src.at[mid_rows], l_in.at[r, mid_rows], l_send.at[r, 0], l_recv.at[r, 0], c + 1, s),
            copy(src.at[low_rows], l_in.at[r, high_rows], l_send.at[r, 1], l_recv.at[r, 1], c + 1, s - 1),
            copy(src.at[high_rows], l_in.at[r, low_rows], l_send.at[r, 2], l_recv.at[r, 2], c + 1, s + 1),
        )

    def product_copy(k, r):
        partner = c + (1 << k) * (1 - 2 * ((c // (1 << k)) % 2))
        return copy(prods.at[k, r], others.at[k, r], k_send.at[k, r], k_recv.at[k, r], partner, s)

    @pl.when(above)
    def _():
        size_up().start()

    @pl.when(below)
    def _():
        size_down().start()

    @pl.when(c == cols - 1)
    def _():
        load_right.wait()
        for r in range(row_count):
            r_in[r, mid_rows, :] = r_out[r]
            _, down, up = right_copies(r, r_out.at[r], c)

            @pl.when(below)
            def _():
                down.start()

            @pl.when(above)
            def _():
                up.start()

    @pl.when(c == 0)
    def _():
        for r in range(row_count):
            l_in[r, low_rows, :] = jnp.zeros((blk, width), F32)
            l_in[r, high_rows, :] = jnp.zeros((blk, width), F32)
        load_left.wait()

    for r in range(row_count):
        product_copy(0, r).start()

    first = lax.broadcasted_iota(jnp.int32, (blk, 2 * blk), 1) < blk
    zero = jnp.zeros((blk, 2 * blk), F32)
    load_a.wait()
    for r in range(row_count):
        parts = [a_ref[r, 0, p] for p in range(3)]
        matrix = jnp.concatenate(
            [
                jnp.where(first, parts[0], zero),
                jnp.where(first, parts[1], parts[0]),
                jnp.where(first, parts[2], parts[1]),
                jnp.where(first, zero, parts[2]),
            ],
            axis=0,
        )
        a_wide[r] = wide(matrix)
        at_tall[r] = jnp.concatenate(split(matrix.T), axis=0)

    @pl.when(below)
    def _():
        size_up().wait_recv()

    @pl.when(above)
    def _():
        size_down().wait_recv()

    place = lax.broadcasted_iota(jnp.int32, (blk, width), 0).astype(F32)
    for b, limit in enumerate((halo_sizes[0:1, :], sizes[0:1, :], sizes[8:9, :], halo_sizes[8:9, :])):
        live = (place < limit).astype(F32)
        for r in range(row_count):
            weight[r, b * blk : (b + 1) * blk, :] = live * norms[r]

    def left_step():
        for r in range(row_count):
            main, down, up = left_copies(r)

            @pl.when(before)
            def _():
                main.wait_recv()

            @pl.when(before & above)
            def _():
                down.wait_recv()

            @pl.when(before & below)
            def _():
                up.wait_recv()

            env = jnp.concatenate(
                [
                    l_in[r, blk : 2 * blk, :] + l_in[r, 0:blk, :],
                    l_in[r, 2 * blk : 3 * blk, :] + l_in[r, 3 * blk : 4 * blk, :],
                ],
                axis=0,
            )
            m_keep[r] = env

            @pl.when(after)
            def _():
                l_out[r] = times(a_wide[r], env) * weight[r]
                @pl.when(below)
                def _():
                    down.start()

                @pl.when(above)
                def _():
                    up.start()

                main.start()

    def right_step():
        for r in range(row_count):
            main, down, up = right_copies(r, r_out.at[r], c - 1)

            @pl.when(after)
            def _():
                main.wait_recv()

            @pl.when(above)
            def _():
                down.wait_recv()

            @pl.when(below)
            def _():
                up.wait_recv()

            env = r_in[r] * weight[r]
            x_keep[r] = env

            @pl.when(before)
            def _():
                @pl.when((c == cols - 1) & below)
                def _():
                    down.wait_send()

                @pl.when((c == cols - 1) & above)
                def _():
                    up.wait_send()

                both = dot(at_tall[r], wide(env), ((1,), (0,)))
                half = both[: 2 * blk] + both[2 * blk :]
                r_out[r] = half[:, :width] + half[:, width:]
                @pl.when(below)
                def _():
                    down.start()

                @pl.when(above)
                def _():
                    up.start()

                main.start()

    def product_round(k):
        upper = (c // (1 << k)) % 2 == 1
        for r in range(row_count):
            product_copy(k, r).wait_recv()
            mine, other = prods[k, r], others[k, r]
            x = jnp.where(upper, other, mine)
            y = jnp.where(upper, mine, other)
            prods[k + 1, r] = times(wide(x), y)
            if k + 1 < rounds:
                product_copy(k + 1, r).start()

    early = c < cols // 2

    def fold():
        @pl.when(early)
        def _():
            for r in range(row_count):
                y_keep[r] = times(wide(m_keep[r]), prods[rounds, r])

        @pl.when(jnp.logical_not(early))
        def _():
            for r in range(row_count):
                x_keep[r] = times_t(wide(x_keep[r]), prods[rounds, r])

    def slot(t, carry):
        @pl.when(c == t)
        def _():
            left_step()

        @pl.when(c == cols - 1 - t)
        def _():
            right_step()

        for k in range(rounds):

            @pl.when(t == 2 + 2 * k)
            def _():
                product_round(k)

        @pl.when(t == cols - 2)
        def _():
            fold()

        return carry

    lax.fori_loop(0, cols, slot, 0)

    scale = 1.0 / math.sqrt(width)
    for r in range(row_count):

        @pl.when(jnp.logical_not(early))
        def _():
            y_keep[r] = m_keep[r]

        full = times_t(wide(x_keep[r]), y_keep[r]) * scale
        for p in range(3):
            out_ref[r, 0, p] = jnp.where(
                first, full[p * blk : (p + 1) * blk], full[(p + 1) * blk : (p + 2) * blk]
            )

    @pl.when(above)
    def _():
        size_up().wait_send()

    @pl.when(below)
    def _():
        size_down().wait_send()

    for r in range(row_count):
        for k in range(rounds):
            product_copy(k, r).wait_send()
        for there, (main, down, up) in (
            (after, left_copies(r)),
            (before, right_copies(r, r_out.at[r], c - 1)),
        ):

            @pl.when(there)
            def _():
                main.wait_send()

            @pl.when(there & below)
            def _():
                down.wait_send()

            @pl.when(there & above)
            def _():
                up.wait_send()


def body(cols, secs, couplings, lower_sites, left_edge, right_edge, bond_sizes):
    row_count, _, _, blk, lanes = couplings.shape
    width = lower_sites.shape[3]
    rounds = cols.bit_length() - 1
    dma = pltpu.SemaphoreType.DMA
    left_edge = left_edge.reshape(row_count, lanes, width)
    right_edge = right_edge.reshape(row_count, lanes, width)
    vmem = pl.BlockSpec(memory_space=pltpu.VMEM)
    return pl.pallas_call(
        functools.partial(kernel, cols, secs),
        out_shape=jax.ShapeDtypeStruct(couplings.shape, F32),
        in_specs=[pl.BlockSpec(memory_space=pltpu.HBM)] * 5,
        out_specs=vmem,
        scratch_shapes=[
            pltpu.VMEM(couplings.shape, F32),
            pltpu.VMEM(lower_sites.shape, F32),
            pltpu.SMEM(bond_sizes.shape, jnp.int32),
            pltpu.VMEM((row_count, 4 * blk, width), F32),
            pltpu.VMEM((row_count, 4 * blk, width), F32),
            pltpu.VMEM((row_count, 4 * blk, width), F32),
            pltpu.VMEM((row_count, 2 * blk, width), F32),
            pltpu.VMEM((row_count, 2 * blk, width), F32),
            pltpu.VMEM((row_count, 4 * blk, width), F32),
            pltpu.VMEM((row_count, 2 * blk, width), F32),
            pltpu.VMEM((row_count, 4 * blk, 2 * lanes), BF16),
            pltpu.VMEM((row_count, 2 * lanes, 4 * blk), BF16),
            pltpu.VMEM((row_count, 4 * blk, width), F32),
            pltpu.VMEM((16, width), F32),
            pltpu.VMEM((16, width), F32),
            pltpu.VMEM((rounds + 1, row_count, width, width), F32),
            pltpu.VMEM((rounds, row_count, width, width), F32),
            dma((row_count, 3)),
            dma((row_count, 3)),
            dma((row_count, 3)),
            dma((row_count, 3)),
            dma((2,)),
            dma((2,)),
            dma((rounds, row_count)),
            dma((rounds, row_count)),
            dma((5,)),
        ],
        compiler_params=pltpu.CompilerParams(
            collective_id=0, has_side_effects=True, vmem_limit_bytes=64 * 1024 * 1024 - 65536
        ),
    )(couplings, lower_sites, left_edge, right_edge, bond_sizes)


def solution(mesh):
    in_specs = (
        P(None, "col", None, None, "sec"),
        P(None, "col", None, None),
        P(None, "sec", None, None),
        P(None, "sec", None, None),
        P("col", "sec"),
    )
    out_specs = P(None, "col", None, None, "sec")
    run = functools.partial(body, mesh.shape["col"], mesh.shape["sec"])
    return jax.shard_map(run, mesh=mesh, in_specs=in_specs, out_specs=out_specs, check_vma=False)
```

```python
import functools
import math

import jax
import jax.numpy as jnp
from jax import lax
from jax.experimental import pallas as pl
from jax.experimental.pallas import tpu as pltpu
from jax.sharding import PartitionSpec as P

MESH = pl.DeviceIdType.MESH
F32 = jnp.float32
BF16 = jnp.bfloat16


def split(x):
    high = x.astype(BF16)
    low = (x - high.astype(F32)).astype(BF16)
    return high, low


def wide(x):
    return jnp.concatenate(split(x), axis=1)


def dot(a, b, contract):
    return lax.dot_general(a, b, (contract, ((), ())), preferred_element_type=F32)


def times(x_wide, y):
    pair = wide(y)
    both = dot(x_wide, jnp.concatenate([pair, pair], axis=0), ((1,), (0,)))
    n = y.shape[1]
    return both[:, :n] + both[:, n:]


def times_t(x_wide, y):
    high, low = split(y)
    rows = jnp.concatenate(
        [jnp.concatenate([high, high], axis=1), jnp.concatenate([low, low], axis=1)], axis=0
    )
    both = dot(x_wide, rows, ((1,), (1,)))
    n = y.shape[0]
    return both[:, :n] + both[:, n:]


def kernel(
    cols, secs, a_hbm, b_hbm, left_hbm, right_hbm, size_hbm, out_ref, a_ref, b_ref, size_ref,
    l_in, r_in, l_out, r_out, m_keep, x_keep, y_keep, a_wide, at_tall, weight, sizes, halo_sizes, halo_a, prods, others,
    l_send, l_recv, r_send, r_recv, h_send, h_recv, a_send, a_recv, k_send, k_recv, local,
):
    row_count = a_ref.shape[0]
    blk = a_ref.shape[3]
    width = b_ref.shape[3]
    rounds = cols.bit_length() - 1
    c = lax.axis_index("col")
    s = lax.axis_index("sec")
    below, above = s > 0, s < secs - 1
    before, after = c > 0, c < cols - 1
    odd = c % 2 == 1
    even = jnp.logical_not(odd)
    low_rows, mid_rows, high_rows = pl.ds(0, 2 * blk), pl.ds(2 * blk, 2 * blk), pl.ds(4 * blk, 2 * blk)
    near_rows = pl.ds(blk, 4 * blk)

    def copy(src, dst, send, recv, dc, ds):
        return pltpu.make_async_remote_copy(
            src_ref=src, dst_ref=dst, send_sem=send, recv_sem=recv,
            device_id=(dc, ds), device_id_type=MESH,
        )

    load_a = pltpu.make_async_copy(a_hbm, a_ref, local.at[0])
    load_b = pltpu.make_async_copy(b_hbm, b_ref, local.at[1])
    load_size = pltpu.make_async_copy(size_hbm, size_ref, local.at[2])
    load_left = pltpu.make_async_copy(left_hbm, l_in.at[:, mid_rows], local.at[3])
    load_right = pltpu.make_async_copy(right_hbm, r_in.at[:, mid_rows], local.at[4])
    load_size.start()
    load_b.start()
    load_a.start()

    @pl.when(c == 0)
    def _():
        load_left.start()

    @pl.when(c == cols - 1)
    def _():
        load_right.start()

    barrier = pltpu.get_barrier_semaphore()
    count = jnp.int32(rounds)
    for k in range(rounds):
        partner = c + (1 << k) * (1 - 2 * ((c // (1 << k)) % 2))
        pl.semaphore_signal(barrier, inc=1, device_id=(partner, s), device_id_type=MESH)
    for dc, there in ((0, None), (-1, before), (1, after)):
        for ds, beside in ((0, None), (-1, below), (1, above)):
            if dc == 0 and ds == 0:
                continue
            if there is None:
                exists = beside
            elif beside is None:
                exists = there
            else:
                exists = there & beside
            count = count + exists.astype(jnp.int32)

            @pl.when(exists)
            def _(dc=dc, ds=ds):
                pl.semaphore_signal(barrier, inc=1, device_id=(c + dc, s + ds), device_id_type=MESH)

    load_size.wait()
    sizes[0:8, :] = jnp.full((8, width), size_ref[0, 0].astype(F32), F32)
    sizes[8:16, :] = jnp.full((8, width), size_ref[0, 1].astype(F32), F32)
    norms = []
    load_b.wait()
    for r in range(row_count):
        lower = b_ref[r, 0]
        norm = jnp.max(jnp.sum(jnp.abs(lower), axis=1, keepdims=True), axis=0, keepdims=True)
        norm = jnp.maximum(norm, 1e-30)
        norms.append(norm)
        prods[0, r] = lower / norm

    def clear(ref, start, length):
        for r in range(row_count):
            ref[r, start : start + length, :] = jnp.zeros((length, width), F32)

    @pl.when(s == 0)
    def _():
        halo_sizes[0] = jnp.zeros((16, width), F32)
        halo_a[0] = jnp.zeros(halo_a.shape[1:], F32)

    @pl.when(s == secs - 1)
    def _():
        halo_sizes[1] = jnp.zeros((16, width), F32)
        halo_a[1] = jnp.zeros(halo_a.shape[1:], F32)

    for near, ref in ((odd, l_in), (even, r_in)):

        @pl.when(near)
        def _(ref=ref):
            clear(ref, 0, blk)
            clear(ref, 5 * blk, blk)

        @pl.when(jnp.logical_not(near) & (s == 0))
        def _(ref=ref):
            clear(ref, 0, 2 * blk)

        @pl.when(jnp.logical_not(near) & (s == secs - 1))
        def _(ref=ref):
            clear(ref, 4 * blk, 2 * blk)

    pl.semaphore_wait(barrier, count)

    def halo_copies(side, to):
        return [copy(sizes, halo_sizes.at[side], h_send.at[side], h_recv.at[side], c, to)] + [
            copy(a_ref.at[r], halo_a.at[side, r], a_send.at[side, r], a_recv.at[side, r], c, to)
            for r in range(row_count)
        ]

    def far_copies(src, dst, send, recv, to):
        return (
            copy(src, dst.at[mid_rows], send.at[0], recv.at[0], to, s),
            copy(src, dst.at[high_rows], send.at[1], recv.at[1], to, s - 1),
            copy(src, dst.at[low_rows], send.at[2], recv.at[2], to, s + 1),
        )

    def near_copy(src, dst, send, recv, to):
        return copy(src, dst.at[near_rows], send.at[0], recv.at[0], to, s)

    class Way:
        def __init__(self, src, dst, send, recv, to):
            self.args = (src, dst, send, recv)
            self.to = to

        def far(self, r, to=None, src=None):
            own, dst, send, recv = (ref.at[r] for ref in self.args)
            src = own.at[pl.ds(blk, 2 * blk)] if src is None else src
            return far_copies(src, dst, send, recv, self.to if to is None else to)

        def near(self, r):
            src, dst, send, recv = (ref.at[r] for ref in self.args)
            return near_copy(src, dst, send, recv, self.to)

    left = Way(l_out, l_in, l_send, l_recv, c + 1)
    right = Way(r_out, r_in, r_send, r_recv, c - 1)

    def edge_copies(way, r):
        return way.far(r, c, way.args[1].at[r, mid_rows])

    def sideways(copies, act, here=None):
        _, down, up = copies
        for exists, one in ((below, down), (above, up)):

            @pl.when(exists if here is None else exists & here)
            def _(one=one):
                act(one)

    def product_copy(k, r):
        partner = c + (1 << k) * (1 - 2 * ((c // (1 << k)) % 2))
        return copy(prods.at[k, r], others.at[k, r], k_send.at[k, r], k_recv.at[k, r], partner, s)

    load_a.wait()

    for k in range(1 + row_count):
        for exists, side, to in ((above, 0, s + 1), (below, 1, s - 1)):

            @pl.when(exists)
            def _(side=side, to=to):
                halo_copies(side, to)[k].start()

        if k > 0:
            for here, load, way in ((c == 0, load_left, left), (c == cols - 1, load_right, right)):

                @pl.when(here)
                def _(load=load, way=way):
                    if k == 1:
                        load.wait()
                    sideways(edge_copies(way, k - 1), lambda one: one.start())

    for r in range(row_count):
        product_copy(0, r).start()

    first = lax.broadcasted_iota(jnp.int32, (blk, 2 * blk), 1) < blk
    zero = jnp.zeros((blk, 2 * blk), F32)

    def spread(of_first, of_second, height):
        return jnp.concatenate([jnp.where(first, of_first(n), of_second(n)) for n in range(height)], axis=0)

    def arrive(k):
        for exists, side, to in ((below, 0, s - 1), (above, 1, s + 1)):

            @pl.when(exists)
            def _(side=side, to=to):
                halo_copies(side, to)[k].wait_recv()

    arrive(0)

    place = lax.broadcasted_iota(jnp.int32, (blk, width), 0).astype(F32)
    limits = [sizes[0:1, :], sizes[8:9, :]]
    limits = [halo_sizes[0, 0:1, :], halo_sizes[0, 8:9, :]] + limits
    limits = limits + [halo_sizes[1, 0:1, :], halo_sizes[1, 8:9, :]]
    for b, limit in enumerate(limits):
        live = (place < limit).astype(F32)
        for r in range(row_count):
            weight[r, b * blk : (b + 1) * blk, :] = live * norms[r]

    def prepare(r):
        arrive(1 + r)

        def part(ref):
            return lambda p: ref[p] if 0 <= p <= 2 else zero

        low, own, high = part(halo_a.at[0, r, 0]), part(a_ref.at[r, 0]), part(halo_a.at[1, r, 0])
        groups = [
            spread(lambda n, g=g, one=one: one(n - 2 * g + 2), lambda n, g=g, one=one: one(n - 2 * g + 1), 4)
            for g, one in enumerate((low, own, high))
        ]
        a_wide[r] = wide(jnp.concatenate(groups, axis=1))
        inner = spread(lambda n: own(n - 1), lambda n: own(n - 2), 6)
        outer = spread(lambda n: high(n - 3), lambda n: low(n), 6)
        at_tall[r] = jnp.concatenate(split(jnp.concatenate([inner.T, outer.T], axis=0)), axis=0)

    def receive(way, r, near, start):
        @pl.when(near)
        def _():
            way.near(r).wait_recv()

        @pl.when(jnp.logical_not(near))
        def _():
            main, down, up = way.far(r)

            @pl.when(jnp.logical_not(start))
            def _():
                main.wait_recv()

            sideways((main, up, down), lambda one: one.wait_recv())

    def send(way, r, near):
        @pl.when(near)
        def _():
            way.near(r).start()

        @pl.when(jnp.logical_not(near))
        def _():
            copies = way.far(r)
            sideways(copies, lambda one: one.start())
            copies[0].start()

    def left_step(rows=range(row_count)):
        for r in rows:
            receive(left, r, odd, c == 0)
            m_keep[r] = l_in[r, mid_rows, :]

            @pl.when(after)
            def _(r=r):
                l_out[r] = times(a_wide[r], l_in[r]) * weight[r, near_rows, :]
                send(left, r, even)

    def right_step(rows=range(row_count)):
        for r in rows:
            receive(right, r, even, c == cols - 1)
            x_keep[r] = r_in[r, near_rows, :] * weight[r, near_rows, :]

            @pl.when(before)
            def _(r=r):
                both = dot(at_tall[r], wide(r_in[r] * weight[r]), ((1,), (0,)))
                half = both[: 4 * blk] + both[4 * blk :]
                half = half[:, :width] + half[:, width:]
                r_out[r, 0:blk, :] = half[3 * blk : 4 * blk]
                r_out[r, blk : 3 * blk, :] = half[0 : 2 * blk]
                r_out[r, 3 * blk : 4 * blk, :] = half[2 * blk : 3 * blk]
                send(right, r, odd)

    def product_round(k):
        upper = (c // (1 << k)) % 2 == 1
        for r in range(row_count):
            product_copy(k, r).wait_recv()
            mine, other = prods[k, r], others[k, r]
            x = jnp.where(upper, other, mine)
            y = jnp.where(upper, mine, other)
            prods[k + 1, r] = times(wide(x), y)
            if k + 1 < rounds:
                product_copy(k + 1, r).start()

    early = c < cols // 2

    def fold():
        @pl.when(early)
        def _():
            for r in range(row_count):
                y_keep[r] = times(wide(m_keep[r]), prods[rounds, r])

        @pl.when(jnp.logical_not(early))
        def _():
            for r in range(row_count):
                x_keep[r] = times_t(wide(x_keep[r]), prods[rounds, r])

    def slot(t, carry):
        @pl.when(c == t)
        def _():
            left_step()

        @pl.when(c == cols - 1 - t)
        def _():
            right_step()

        for k in range(rounds):

            @pl.when(t == 2 + 2 * k)
            def _():
                product_round(k)

        @pl.when(t == cols - 2)
        def _():
            fold()

        return carry

    for r in range(row_count):
        prepare(r)

        @pl.when(c == 0)
        def _(r=r):
            left_step([r])

        @pl.when(c == cols - 1)
        def _(r=r):
            right_step([r])

    lax.fori_loop(1, cols, slot, 0)

    scale = 1.0 / math.sqrt(width)
    for r in range(row_count):

        @pl.when(jnp.logical_not(early))
        def _():
            y_keep[r] = m_keep[r]

        full = times_t(wide(x_keep[r]), y_keep[r]) * scale
        for p in range(3):
            out_ref[r, 0, p] = jnp.where(
                first, full[p * blk : (p + 1) * blk], full[(p + 1) * blk : (p + 2) * blk]
            )

    for exists, side, to in ((above, 0, s + 1), (below, 1, s - 1)):

        @pl.when(exists)
        def _(side=side, to=to):
            for one in halo_copies(side, to):
                one.wait_send()

    for r in range(row_count):
        for k in range(rounds):
            product_copy(k, r).wait_send()
        for way, near, start, there in ((left, even, c == 0, after), (right, odd, c == cols - 1, before)):

            @pl.when(near & there)
            def _(way=way):
                way.near(r).wait_send()

            @pl.when(start)
            def _(way=way):
                sideways(edge_copies(way, r), lambda one: one.wait_send())

            @pl.when(jnp.logical_not(near) & there)
            def _(way=way):
                copies = way.far(r)
                copies[0].wait_send()
                sideways(copies, lambda one: one.wait_send())


def body(cols, secs, couplings, lower_sites, left_edge, right_edge, bond_sizes):
    row_count, _, _, blk, lanes = couplings.shape
    width = lower_sites.shape[3]
    rounds = cols.bit_length() - 1
    dma = pltpu.SemaphoreType.DMA
    left_edge = left_edge.reshape(row_count, lanes, width)
    right_edge = right_edge.reshape(row_count, lanes, width)
    vmem = pl.BlockSpec(memory_space=pltpu.VMEM)
    return pl.pallas_call(
        functools.partial(kernel, cols, secs),
        out_shape=jax.ShapeDtypeStruct(couplings.shape, F32),
        in_specs=[pl.BlockSpec(memory_space=pltpu.HBM)] * 5,
        out_specs=vmem,
        scratch_shapes=[
            pltpu.VMEM(couplings.shape, F32),
            pltpu.VMEM(lower_sites.shape, F32),
            pltpu.SMEM(bond_sizes.shape, jnp.int32),
            pltpu.VMEM((row_count, 6 * blk, width), F32),
            pltpu.VMEM((row_count, 6 * blk, width), F32),
            pltpu.VMEM((row_count, 4 * blk, width), F32),
            pltpu.VMEM((row_count, 4 * blk, width), F32),
            pltpu.VMEM((row_count, 2 * blk, width), F32),
            pltpu.VMEM((row_count, 4 * blk, width), F32),
            pltpu.VMEM((row_count, 2 * blk, width), F32),
            pltpu.VMEM((row_count, 4 * blk, 6 * lanes), BF16),
            pltpu.VMEM((row_count, 4 * lanes, 6 * blk), BF16),
            pltpu.VMEM((row_count, 6 * blk, width), F32),
            pltpu.VMEM((16, width), F32),
            pltpu.VMEM((2, 16, width), F32),
            pltpu.VMEM((2,) + couplings.shape, F32),
            pltpu.VMEM((rounds + 1, row_count, width, width), F32),
            pltpu.VMEM((rounds, row_count, width, width), F32),
            dma((row_count, 3)),
            dma((row_count, 3)),
            dma((row_count, 3)),
            dma((row_count, 3)),
            dma((2,)),
            dma((2,)),
            dma((2, row_count)),
            dma((2, row_count)),
            dma((rounds, row_count)),
            dma((rounds, row_count)),
            dma((5,)),
        ],
        compiler_params=pltpu.CompilerParams(
            collective_id=0, has_side_effects=True, vmem_limit_bytes=64 * 1024 * 1024 - 65536
        ),
    )(couplings, lower_sites, left_edge, right_edge, bond_sizes)


def solution(mesh):
    in_specs = (
        P(None, "col", None, None, "sec"),
        P(None, "col", None, None),
        P(None, "sec", None, None),
        P(None, "sec", None, None),
        P("col", "sec"),
    )
    out_specs = P(None, "col", None, None, "sec")
    run = functools.partial(body, mesh.shape["col"], mesh.shape["sec"])
    return jax.shard_map(run, mesh=mesh, in_specs=in_specs, out_specs=out_specs, check_vma=False)
```

```python
import functools
import math

import jax
import jax.numpy as jnp
from jax import lax
from jax.experimental import pallas as pl
from jax.experimental.pallas import tpu as pltpu
from jax.sharding import PartitionSpec as P

MESH = pl.DeviceIdType.MESH
F32 = jnp.float32
BF16 = jnp.bfloat16


def split(x):
    high = x.astype(BF16)
    low = (x - high.astype(F32)).astype(BF16)
    return high, low


def wide(x):
    return jnp.concatenate(split(x), axis=1)


def dot(a, b, contract):
    return lax.dot_general(a, b, (contract, ((), ())), preferred_element_type=F32)


def times(x_wide, y):
    pair = wide(y)
    both = dot(x_wide, jnp.concatenate([pair, pair], axis=0), ((1,), (0,)))
    n = y.shape[1]
    return both[:, :n] + both[:, n:]


def times_t(x_wide, y):
    high, low = split(y)
    rows = jnp.concatenate(
        [jnp.concatenate([high, high], axis=1), jnp.concatenate([low, low], axis=1)], axis=0
    )
    both = dot(x_wide, rows, ((1,), (1,)))
    n = y.shape[0]
    return both[:, :n] + both[:, n:]


def kernel(
    cols, secs, a_hbm, b_hbm, left_hbm, right_hbm, size_hbm, out_ref, a_ref, b_ref, size_ref,
    l_in, r_in, l_out, r_out, m_keep, x_keep, y_keep, a_wide, at_tall, weight, sizes, halo_sizes, prods, others,
    l_send, l_recv, r_send, r_recv, h_send, h_recv, k_send, k_recv, local,
):
    row_count = a_ref.shape[0]
    blk = a_ref.shape[3]
    width = b_ref.shape[3]
    rounds = cols.bit_length() - 1
    c = lax.axis_index("col")
    s = lax.axis_index("sec")
    below, above = s > 0, s < secs - 1
    before, after = c > 0, c < cols - 1
    low_rows, mid_rows, high_rows = pl.ds(0, blk), pl.ds(blk, 2 * blk), pl.ds(3 * blk, blk)

    def copy(src, dst, send, recv, dc, ds):
        return pltpu.make_async_remote_copy(
            src_ref=src, dst_ref=dst, send_sem=send, recv_sem=recv,
            device_id=(dc, ds), device_id_type=MESH,
        )

    load_a = pltpu.make_async_copy(a_hbm, a_ref, local.at[0])
    load_b = pltpu.make_async_copy(b_hbm, b_ref, local.at[1])
    load_size = pltpu.make_async_copy(size_hbm, size_ref, local.at[2])
    load_left = pltpu.make_async_copy(left_hbm, l_in.at[:, mid_rows], local.at[3])
    load_right = pltpu.make_async_copy(right_hbm, r_out, local.at[4])
    load_size.start()
    load_b.start()
    load_a.start()

    @pl.when(c == 0)
    def _():
        load_left.start()

    @pl.when(c == cols - 1)
    def _():
        load_right.start()

    barrier = pltpu.get_barrier_semaphore()
    count = jnp.int32(rounds)
    for k in range(rounds):
        partner = c + (1 << k) * (1 - 2 * ((c // (1 << k)) % 2))
        pl.semaphore_signal(barrier, inc=1, device_id=(partner, s), device_id_type=MESH)
    for dc, there in ((0, None), (-1, before), (1, after)):
        for ds, beside in ((0, None), (-1, below), (1, above)):
            if dc == 0 and ds == 0:
                continue
            if there is None:
                exists = beside
            elif beside is None:
                exists = there
            else:
                exists = there & beside
            count = count + exists.astype(jnp.int32)

            @pl.when(exists)
            def _(dc=dc, ds=ds):
                pl.semaphore_signal(barrier, inc=1, device_id=(c + dc, s + ds), device_id_type=MESH)

    load_size.wait()
    sizes[0:8, :] = jnp.full((8, width), size_ref[0, 0].astype(F32), F32)
    sizes[8:16, :] = jnp.full((8, width), size_ref[0, 1].astype(F32), F32)
    norms = []
    load_b.wait()
    for r in range(row_count):
        lower = b_ref[r, 0]
        norm = jnp.max(jnp.sum(jnp.abs(lower), axis=1, keepdims=True), axis=0, keepdims=True)
        norm = jnp.maximum(norm, 1e-30)
        norms.append(norm)
        prods[0, r] = lower / norm

    @pl.when(s == 0)
    def _():
        halo_sizes[0:8, :] = jnp.zeros((8, width), F32)
        r_in[:, low_rows, :] = jnp.zeros((row_count, blk, width), F32)
        l_in[:, low_rows, :] = jnp.zeros((row_count, blk, width), F32)

    @pl.when(s == secs - 1)
    def _():
        halo_sizes[8:16, :] = jnp.zeros((8, width), F32)
        r_in[:, high_rows, :] = jnp.zeros((row_count, blk, width), F32)
        l_in[:, high_rows, :] = jnp.zeros((row_count, blk, width), F32)

    pl.semaphore_wait(barrier, count)

    def size_up():
        return copy(sizes.at[8:16], halo_sizes.at[0:8], h_send.at[0], h_recv.at[0], c, s + 1)

    def size_down():
        return copy(sizes.at[0:8], halo_sizes.at[8:16], h_send.at[1], h_recv.at[1], c, s - 1)

    def right_copies(r, src, dc):
        return (
            copy(src.at[pl.ds(0, 2 * blk)], r_in.at[r, mid_rows], r_send.at[r, 0], r_recv.at[r, 0], dc, s),
            copy(src.at[pl.ds(0, blk)], r_in.at[r, high_rows], r_send.at[r, 1], r_recv.at[r, 1], dc, s - 1),
            copy(src.at[pl.ds(blk, blk)], r_in.at[r, low_rows], r_send.at[r, 2], r_recv.at[r, 2], dc, s + 1),
        )

    def left_copies(r):
        src = l_out.at[r]
        return (
            copy(src.at[mid_rows], l_in.at[r, mid_rows], l_send.at[r, 0], l_recv.at[r, 0], c + 1, s),
            copy(src.at[low_rows], l_in.at[r, high_rows], l_send.at[r, 1], l_recv.at[r, 1], c + 1, s - 1),
            copy(src.at[high_rows], l_in.at[r, low_rows], l_send.at[r, 2], l_recv.at[r, 2], c + 1, s + 1),
        )

    def product_copy(k, r):
        partner = c + (1 << k) * (1 - 2 * ((c // (1 << k)) % 2))
        return copy(prods.at[k, r], others.at[k, r], k_send.at[k, r], k_recv.at[k, r], partner, s)

    @pl.when(above)
    def _():
        size_up().start()

    @pl.when(below)
    def _():
        size_down().start()

    @pl.when(c == cols - 1)
    def _():
        load_right.wait()
        for r in range(row_count):
            r_in[r, mid_rows, :] = r_out[r]
            _, down, up = right_copies(r, r_out.at[r], c)

            @pl.when(below)
            def _():
                down.start()

            @pl.when(above)
            def _():
                up.start()

    @pl.when(c == 0)
    def _():
        for r in range(row_count):
            l_in[r, low_rows, :] = jnp.zeros((blk, width), F32)
            l_in[r, high_rows, :] = jnp.zeros((blk, width), F32)
        load_left.wait()

    for r in range(row_count):
        product_copy(0, r).start()

    first = lax.broadcasted_iota(jnp.int32, (blk, 2 * blk), 1) < blk
    zero = jnp.zeros((blk, 2 * blk), F32)
    load_a.wait()
    for r in range(row_count):
        parts = [a_ref[r, 0, p] for p in range(3)]
        matrix = jnp.concatenate(
            [
                jnp.where(first, parts[0], zero),
                jnp.where(first, parts[1], parts[0]),
                jnp.where(first, parts[2], parts[1]),
                jnp.where(first, zero, parts[2]),
            ],
            axis=0,
        )
        a_wide[r] = wide(matrix)
        at_tall[r] = jnp.concatenate(split(matrix.T), axis=0)

    @pl.when(below)
    def _():
        size_up().wait_recv()

    @pl.when(above)
    def _():
        size_down().wait_recv()

    place = lax.broadcasted_iota(jnp.int32, (blk, width), 0).astype(F32)
    for b, limit in enumerate((halo_sizes[0:1, :], sizes[0:1, :], sizes[8:9, :], halo_sizes[8:9, :])):
        live = (place < limit).astype(F32)
        for r in range(row_count):
            weight[r, b * blk : (b + 1) * blk, :] = live * norms[r]

    def left_step():
        for r in range(row_count):
            main, down, up = left_copies(r)

            @pl.when(before)
            def _():
                main.wait_recv()

            @pl.when(before & above)
            def _():
                down.wait_recv()

            @pl.when(before & below)
            def _():
                up.wait_recv()

            env = jnp.concatenate(
                [
                    l_in[r, blk : 2 * blk, :] + l_in[r, 0:blk, :],
                    l_in[r, 2 * blk : 3 * blk, :] + l_in[r, 3 * blk : 4 * blk, :],
                ],
                axis=0,
            )
            m_keep[r] = env

            @pl.when(after)
            def _():
                l_out[r] = times(a_wide[r], env) * weight[r]
                @pl.when(below)
                def _():
                    down.start()

                @pl.when(above)
                def _():
                    up.start()

                main.start()

    def right_step():
        for r in range(row_count):
            main, down, up = right_copies(r, r_out.at[r], c - 1)

            @pl.when(after)
            def _():
                main.wait_recv()

            @pl.when(above)
            def _():
                down.wait_recv()

            @pl.when(below)
            def _():
                up.wait_recv()

            env = r_in[r] * weight[r]
            x_keep[r] = env

            @pl.when(before)
            def _():
                @pl.when((c == cols - 1) & below)
                def _():
                    down.wait_send()

                @pl.when((c == cols - 1) & above)
                def _():
                    up.wait_send()

                both = dot(at_tall[r], wide(env), ((1,), (0,)))
                half = both[: 2 * blk] + both[2 * blk :]
                r_out[r] = half[:, :width] + half[:, width:]
                @pl.when(below)
                def _():
                    down.start()

                @pl.when(above)
                def _():
                    up.start()

                main.start()

    def product_round(k):
        upper = (c // (1 << k)) % 2 == 1
        for r in range(row_count):
            product_copy(k, r).wait_recv()
            mine, other = prods[k, r], others[k, r]
            x = jnp.where(upper, other, mine)
            y = jnp.where(upper, mine, other)
            prods[k + 1, r] = times(wide(x), y)
            if k + 1 < rounds:
                product_copy(k + 1, r).start()

    early = c < cols // 2

    def fold():
        @pl.when(early)
        def _():
            for r in range(row_count):
                y_keep[r] = times(wide(m_keep[r]), prods[rounds, r])

        @pl.when(jnp.logical_not(early))
        def _():
            for r in range(row_count):
                x_keep[r] = times_t(wide(x_keep[r]), prods[rounds, r])

    def slot(t, carry):
        @pl.when(c == t)
        def _():
            left_step()

        @pl.when(c == cols - 1 - t)
        def _():
            right_step()

        for k in range(rounds):

            @pl.when(t == 2 + 2 * k)
            def _():
                product_round(k)

        @pl.when(t == cols - 2)
        def _():
            fold()

        return carry

    lax.fori_loop(0, cols, slot, 0)

    for r in range(row_count):

        @pl.when(jnp.logical_not(early))
        def _():
            y_keep[r] = m_keep[r]

        full = times_t(wide(x_keep[r]), y_keep[r])
        for p in range(3):
            out_ref[r, 0, p] = jnp.where(
                first, full[p * blk : (p + 1) * blk], full[(p + 1) * blk : (p + 2) * blk]
            )

    @pl.when(above)
    def _():
        size_up().wait_send()

    @pl.when(below)
    def _():
        size_down().wait_send()

    for r in range(row_count):
        for k in range(rounds):
            product_copy(k, r).wait_send()
        for there, (main, down, up) in (
            (after, left_copies(r)),
            (before, right_copies(r, r_out.at[r], c - 1)),
        ):

            @pl.when(there)
            def _():
                main.wait_send()

            @pl.when(there & below)
            def _():
                down.wait_send()

            @pl.when(there & above)
            def _():
                up.wait_send()


def body(cols, secs, couplings, lower_sites, left_edge, right_edge, bond_sizes):
    row_count, _, _, blk, lanes = couplings.shape
    width = lower_sites.shape[3]
    rounds = cols.bit_length() - 1
    dma = pltpu.SemaphoreType.DMA
    left_edge = left_edge.reshape(row_count, lanes, width)
    right_edge = right_edge.reshape(row_count, lanes, width)
    vmem = pl.BlockSpec(memory_space=pltpu.VMEM)
    gradient = pl.pallas_call(
        functools.partial(kernel, cols, secs),
        out_shape=jax.ShapeDtypeStruct(couplings.shape, F32),
        in_specs=[pl.BlockSpec(memory_space=pltpu.HBM)] * 5,
        out_specs=vmem,
        scratch_shapes=[
            pltpu.VMEM(couplings.shape, F32),
            pltpu.VMEM(lower_sites.shape, F32),
            pltpu.SMEM(bond_sizes.shape, jnp.int32),
            pltpu.VMEM((row_count, 4 * blk, width), F32),
            pltpu.VMEM((row_count, 4 * blk, width), F32),
            pltpu.VMEM((row_count, 4 * blk, width), F32),
            pltpu.VMEM((row_count, 2 * blk, width), F32),
            pltpu.VMEM((row_count, 2 * blk, width), F32),
            pltpu.VMEM((row_count, 4 * blk, width), F32),
            pltpu.VMEM((row_count, 2 * blk, width), F32),
            pltpu.VMEM((row_count, 4 * blk, 2 * lanes), BF16),
            pltpu.VMEM((row_count, 2 * lanes, 4 * blk), BF16),
            pltpu.VMEM((row_count, 4 * blk, width), F32),
            pltpu.VMEM((16, width), F32),
            pltpu.VMEM((16, width), F32),
            pltpu.VMEM((rounds + 1, row_count, width, width), F32),
            pltpu.VMEM((rounds, row_count, width, width), F32),
            dma((row_count, 3)),
            dma((row_count, 3)),
            dma((row_count, 3)),
            dma((row_count, 3)),
            dma((2,)),
            dma((2,)),
            dma((rounds, row_count)),
            dma((rounds, row_count)),
            dma((5,)),
        ],
        compiler_params=pltpu.CompilerParams(
            collective_id=0, has_side_effects=True, vmem_limit_bytes=64 * 1024 * 1024 - 65536
        ),
    )(couplings, lower_sites, left_edge, right_edge, bond_sizes)
    return gradient * (1.0 / math.sqrt(width))


def solution(mesh):
    in_specs = (
        P(None, "col", None, None, "sec"),
        P(None, "col", None, None),
        P(None, "sec", None, None),
        P(None, "sec", None, None),
        P("col", "sec"),
    )
    out_specs = P(None, "col", None, None, "sec")
    run = functools.partial(body, mesh.shape["col"], mesh.shape["sec"])
    return jax.shard_map(run, mesh=mesh, in_specs=in_specs, out_specs=out_specs, check_vma=False)
```
